512 devices in a mesh: date: 32 (over y, z_lo), tile: 16 (over x, z_hi, core).
Axes of the slice: x: 4, y: 4, z: 16 (z_hi: 2, z_lo: 8; z = z_hi * 8 + z_lo), core: 2. Of those that a mesh axis runs over, the one named last changes fastest.
Arguments:
- slc: bfloat16 [2, 256, 128, 1024], P(None, 'date', None, 'tile'), may hold values from -40 to 40
Outputs:
- coherence: float32 [2, 256, 512, 256], P(None, 'date', 'tile')
The draws below stay inside these ranges and needn't reach their ends.
All inputs are finite; a program needn't handle non-finite values.
Results may differ from the reference program's by a relative error of at most 0.0003.
Values may be sent and summed in bfloat16 or wider, within the bound.
No kernel may reach another device: no remote copies, remote signals or barrier semaphores. Data moves between devices by JAX's collectives and lax.ppermute only.
A program may use at most 64 MiB of HBM per device.

```python
import math
import jax
import jax.numpy as jnp
from jax import lax

DATE_DEV = 8
COLS = 1024
LOOK_ROWS = 8
LOOK_COLS = 32
DATES = 256
ROWS = 128
N_DATE = 32


def draw_slc(key, part):
    keys = jax.random.split(key, 6)
    shape = (2, DATES, ROWS, COLS)
    common = jnp.clip(jax.random.normal(keys[0], (2, 1, ROWS, COLS), jnp.float32), -5.0, 5.0)
    noise = jnp.clip(jax.random.normal(keys[1], shape, jnp.float32), -5.0, 5.0)
    amplitude = jnp.exp(jax.random.uniform(keys[3], (1, 1, ROWS, COLS), jnp.float32, -1.2, 1.2))
    sigma = jnp.exp(jax.random.uniform(keys[2], (1, DATES, 1, 1), jnp.float32, -0.8, 0.8))
    slope = jax.random.uniform(keys[4], (DATES,), jnp.float32, -3.0, 3.0)
    offset = jax.random.uniform(keys[5], (DATES,), jnp.float32, -math.pi, math.pi)
    columns = jnp.arange(COLS, dtype=jnp.float32) / float(COLS)
    theta = offset[:, None] + 2.0 * math.pi * slope[:, None] * columns[None, :]
    cosine = jnp.cos(theta)[None, :, None, :]
    sine = jnp.sin(theta)[None, :, None, :]
    base = common + sigma * noise
    real_part = base[0] * cosine[0] - base[1] * sine[0]
    imag_part = base[0] * sine[0] + base[1] * cosine[0]
    result = 0.5 * amplitude * jnp.stack([real_part, imag_part])
    return result.astype(jnp.bfloat16)


def setup_inputs(seed: int = 0) -> dict:
    arg_keys = jax.random.split(jax.random.key(seed), 2)
    slc = draw_slc(jax.random.fold_in(arg_keys[1], 71), 0)
    return {"slc": slc}


def looked(data):
    lead, count, rows, cols = data.shape
    shaped = data.reshape(lead, count, rows // LOOK_ROWS, LOOK_ROWS, cols // LOOK_COLS, LOOK_COLS)
    shaped = shaped.transpose(0, 1, 2, 4, 3, 5)
    return shaped.reshape(lead, count, rows // LOOK_ROWS * (cols // LOOK_COLS), LOOK_ROWS * LOOK_COLS)

def pair_block(mine, mine_power, other, other_power):
    area = float(LOOK_ROWS * LOOK_COLS)
    real_real = jnp.einsum('ack,bck->acb', mine[0], other[0])
    imag_imag = jnp.einsum('ack,bck->acb', mine[1], other[1])
    imag_real = jnp.einsum('ack,bck->acb', mine[1], other[0])
    real_imag = jnp.einsum('ack,bck->acb', mine[0], other[1])
    cross = jnp.stack([real_real + imag_imag, imag_real - real_imag]) / area
    scale = jnp.sqrt(mine_power[:, :, None] * other_power.T[None, :, :] + 1e-06)
    return cross / scale[None]

def reference(slc):
    blocks = looked(slc.astype(jnp.float32))
    power = lax.optimization_barrier(jnp.sum(blocks * blocks, axis=(0, 3))) / float(LOOK_ROWS * LOOK_COLS)

    def one_block(start):
        mine = lax.dynamic_slice_in_dim(blocks, start, DATE_DEV, 1)
        mine_power = lax.dynamic_slice_in_dim(power, start, DATE_DEV, 0)
        return pair_block(mine, mine_power, blocks, power)
    starts = jnp.arange(N_DATE, dtype=jnp.int32) * DATE_DEV
    result = lax.map(one_block, starts)
    result = result.transpose(1, 0, 2, 3, 4)
    return result.reshape(2, DATES, result.shape[3], DATES)
```

```python
import jax
import jax.numpy as jnp
from jax import lax
from jax.experimental import pallas as pl
from jax.experimental.pallas import tpu as pltpu
from jax.sharding import PartitionSpec as P

LOOK_ROWS = 8
LOOK_COLS = 32
AREA = float(LOOK_ROWS * LOOK_COLS)
SHIFT = 14.0
DEEPEST = 100.0

VMEM = pl.BlockSpec(memory_space=pltpu.VMEM)


def exchange(x, dates):
    rows = lax.broadcasted_iota(jnp.int32, x.shape, 0)
    lanes = lax.broadcasted_iota(jnp.int32, x.shape, 1)
    height, width = x.shape
    step = dates // 2
    while step:
        low_row = (rows & step) == 0
        low_lane = (lanes & (step * LOOK_COLS)) == 0
        up = pltpu.roll(pltpu.roll(x, height - step, 0), step * LOOK_COLS, 1)
        down = pltpu.roll(pltpu.roll(x, step, 0), width - step * LOOK_COLS, 1)
        x = jnp.where(low_row == low_lane, x, jnp.where(low_row, up, down))
        step //= 2
    return x


def split_looks(x_ref, y_ref):
    parts, dates, cols, rows = x_ref.shape
    for part in range(parts):
        for look in range(cols // LOOK_COLS):
            block = x_ref[part, :, look * LOOK_COLS : (look + 1) * LOOK_COLS, :]
            block = block.reshape(dates * LOOK_COLS, rows).astype(jnp.float32)
            block = exchange(block.T, dates)
            block = block.reshape(rows // LOOK_ROWS, dates, dates * LOOK_COLS)
            y_ref[:, look, part * dates : (part + 1) * dates, :] = block.astype(y_ref.dtype)


def pairs(x_ref, y_ref):
    blocks, both, pixels = x_ref.shape
    dates = both // 2
    count = blocks * dates
    x = x_ref[...].astype(jnp.float32)
    real = x[:, :dates].reshape(count, pixels).astype(jnp.bfloat16)
    imag = x[:, dates:].reshape(count, pixels).astype(jnp.bfloat16)
    one = jnp.concatenate([real, imag], axis=1)
    turned = jnp.concatenate([imag, -real], axis=1)
    dims = (((1,), (1,)), ((), ()))
    cross_real = lax.dot_general(one, one, dims, preferred_element_type=jnp.float32) / AREA
    cross_imag = lax.dot_general(turned, one, dims, preferred_element_type=jnp.float32) / AREA
    i = lax.broadcasted_iota(jnp.int32, (count, count), 0)
    j = lax.broadcasted_iota(jnp.int32, (count, count), 1)
    own = i == j
    diagonal = jnp.where(own, cross_real, 0.0)
    power_i = jnp.sum(diagonal, axis=1, keepdims=True)
    power_j = jnp.sum(diagonal, axis=0, keepdims=True)
    highest = power_i * jnp.max(power_j, axis=1, keepdims=True)
    bound = highest * lax.rsqrt(highest * (highest + 1e-06) + 1e-37)
    depth = jnp.clip(jnp.floor(-0.5 * jnp.log2(bound + 1e-37)), 0.0, DEEPEST)
    scale = lax.rsqrt(power_i * power_j + 1e-06) * jnp.exp2(depth + SHIFT)
    out_real = cross_real * scale
    out_imag = jnp.where(own, depth, cross_imag * scale)
    out = jnp.concatenate(
        [out_real.reshape(blocks, dates, count), out_imag.reshape(blocks, dates, count)], axis=1
    )
    y_ref[...] = out


def spread(x_ref, y_ref):
    looks, both, count = x_ref.shape
    dates = both // 2
    x = x_ref[...]
    first = lax.axis_index("date") * dates
    shape = (looks, dates, count)
    i = lax.broadcasted_iota(jnp.int32, shape, 1)
    j = lax.broadcasted_iota(jnp.int32, shape, 2)
    own = j == i + first
    imag = x[:, dates:]
    depth = jnp.sum(jnp.where(own, imag, 0.0), axis=2, keepdims=True)
    scale = jnp.exp2(-SHIFT - depth)
    y_ref[0] = jnp.swapaxes(x[:, :dates] * scale, 0, 1)
    y_ref[1] = jnp.swapaxes(jnp.where(own, 0.0, imag * scale), 0, 1)


def call(kernel, shape, dtype, x):
    return pl.pallas_call(
        kernel,
        out_shape=jax.ShapeDtypeStruct(shape, dtype),
        in_specs=[VMEM],
        out_specs=VMEM,
        compiler_params=pltpu.CompilerParams(vmem_limit_bytes=32 * 1024 * 1024),
    )(x)


def on_device(slc):
    parts, dates, rows, cols = slc.shape
    blocks = lax.axis_size("date")
    look_rows, looks, pixels = rows // LOOK_ROWS, cols // LOOK_COLS, LOOK_ROWS * LOOK_COLS
    count = blocks * dates
    x = slc.transpose(0, 1, 3, 2)
    x = call(split_looks, (look_rows, looks, parts * dates, pixels), jnp.bfloat16, x)
    x = lax.all_to_all(x, "tile", 0, 0, tiled=True)
    x = x.reshape(blocks, parts * dates, pixels)
    x = lax.all_to_all(x, "date", 0, 0, tiled=True)
    x = call(pairs, (blocks, parts * dates, count), jnp.float32, x)
    x = lax.all_to_all(x.astype(jnp.float16), "date", 0, 0, tiled=True).astype(jnp.float32)
    return call(spread, (parts, dates, blocks, count), jnp.float32, x)


def solution(mesh):
    in_specs = (P(None, "date", None, "tile"),)
    out_specs = P(None, "date", "tile", None)
    return jax.shard_map(
        on_device, mesh=mesh, in_specs=in_specs, out_specs=out_specs, check_vma=False
    )
```

```python
import jax
import jax.numpy as jnp
from jax import lax
from jax.experimental import pallas as pl
from jax.experimental.pallas import tpu as pltpu
from jax.sharding import PartitionSpec as P

LOOK_ROWS = 8
LOOK_COLS = 32
AREA = float(LOOK_ROWS * LOOK_COLS)
SHIFT = 14.0
DEEPEST = 100.0
EXTRA = 16

VMEM = pl.BlockSpec(memory_space=pltpu.VMEM)


def place(cross, flip, half):
    return jnp.where(cross == 1, half * 6 + flip, 2 + half * 2 + flip)


def worked_at(look_row, half, tile):
    y = (look_row // 4 - tile // 4) % 4
    return y * 8 + place((look_row // 2 % 2) ^ (tile // 2 % 2), (look_row % 2) ^ (tile % 2), half)


def found_at(look_col, tile):
    source, half = look_col // 2, look_col % 2
    cross = (source // 2 % 2) ^ (tile // 2 % 2)
    z_lo = place(cross, (source % 2) ^ (tile % 2), half)
    return (tile // 4 - source // 4) % 4 * 8 + jnp.where(cross == 1, 7 - z_lo, z_lo)


def moves():
    pairs = []
    for y in range(4):
        for z_lo in range(8):
            cross = int(z_lo in (0, 1, 6, 7))
            flip = z_lo % 2
            for x in range(4):
                for z_hi in range(2):
                    for core in range(2):
                        here = (y * 8 + z_lo) * 16 + x * 4 + z_hi * 2 + core
                        date = y * 8 + (7 - z_lo if cross else z_lo)
                        tile = (x + y) % 4 * 4 + (z_hi ^ cross) * 2 + (core ^ flip)
                        pairs.append((here, date * 16 + tile))
    return pairs


def exchange(x, dates):
    rows = lax.broadcasted_iota(jnp.int32, x.shape, 0)
    lanes = lax.broadcasted_iota(jnp.int32, x.shape, 1)
    height, width = x.shape
    step = dates // 2
    while step:
        low_row = (rows & step) == 0
        low_lane = (lanes & (step * LOOK_COLS)) == 0
        up = pltpu.roll(pltpu.roll(x, height - step, 0), step * LOOK_COLS, 1)
        down = pltpu.roll(pltpu.roll(x, step, 0), width - step * LOOK_COLS, 1)
        x = jnp.where(low_row == low_lane, x, jnp.where(low_row, up, down))
        step //= 2
    return x


def split_looks(x_ref, y_ref):
    parts, dates, cols, rows = x_ref.shape
    look_rows = rows // LOOK_ROWS
    tile = lax.axis_index("tile")
    for half in range(cols // LOOK_COLS):
        blocks = []
        for part in range(parts):
            block = x_ref[part, :, half * LOOK_COLS : (half + 1) * LOOK_COLS, :]
            block = block.reshape(dates * LOOK_COLS, rows).astype(jnp.float32)
            block = exchange(block.T, dates)
            blocks.append(block.reshape(look_rows, dates, dates * LOOK_COLS))
        looks = jnp.concatenate(blocks, axis=1).astype(y_ref.dtype)
        for look_row in range(look_rows):
            y_ref[worked_at(look_row, half, tile)] = looks[look_row]


def pairs(x_ref, y_ref):
    blocks, both, pixels = x_ref.shape
    dates = both // 2
    count = blocks * dates
    x = x_ref[...].astype(jnp.float32)
    real = x[:, :dates].reshape(count, pixels).astype(jnp.bfloat16)
    imag = x[:, dates:].reshape(count, pixels).astype(jnp.bfloat16)
    one = jnp.concatenate([real, imag], axis=1)
    turned = jnp.concatenate([imag, -real], axis=1)
    dims = (((1,), (1,)), ((), ()))
    cross_real = lax.dot_general(one, one, dims, preferred_element_type=jnp.float32) / AREA
    cross_imag = lax.dot_general(turned, one, dims, preferred_element_type=jnp.float32) / AREA
    i = lax.broadcasted_iota(jnp.int32, (count, count), 0)
    j = lax.broadcasted_iota(jnp.int32, (count, count), 1)
    diagonal = jnp.where(i == j, cross_real, 0.0)
    power_i = jnp.sum(diagonal, axis=1, keepdims=True)
    power_j = jnp.sum(diagonal, axis=0, keepdims=True)
    highest = jnp.max(power_j, axis=1, keepdims=True)
    bound = highest * lax.rsqrt(highest * highest + 1e-06)
    depth = jnp.clip(jnp.floor(-jnp.log2(bound + 1e-37)), 0.0, DEEPEST)
    scale = lax.rsqrt(power_i * power_j + 1e-06) * jnp.exp2(depth + SHIFT)
    y_ref[:count] = jnp.where(i >= j, cross_real, cross_imag) * scale
    y_ref[count:] = jnp.broadcast_to(depth, (EXTRA, count))


def unfold(x_ref, y_ref):
    blocks, both, count = y_ref.shape
    dates = both // 2
    x = x_ref[:count]
    depth = x_ref[count : count + 1]
    turned = x.T
    i = lax.broadcasted_iota(jnp.int32, (count, count), 0)
    j = lax.broadcasted_iota(jnp.int32, (count, count), 1)
    real = jnp.where(i >= j, x, turned)
    imag = jnp.where(i > j, -turned, jnp.where(i == j, depth, x))
    y_ref[:, :dates] = real.reshape(blocks, dates, count)
    y_ref[:, dates:] = imag.reshape(blocks, dates, count)


def spread(x_ref, y_ref):
    looks, both, count = x_ref.shape
    dates = both // 2
    tile = lax.axis_index("tile")
    x = jnp.stack([x_ref[found_at(look, tile)] for look in range(looks)])
    first = lax.axis_index("date") * dates
    shape = (looks, dates, count)
    i = lax.broadcasted_iota(jnp.int32, shape, 1)
    j = lax.broadcasted_iota(jnp.int32, shape, 2)
    own = j == i + first
    imag = x[:, dates:]
    depth = jnp.sum(jnp.where(own, imag, 0.0), axis=2, keepdims=True)
    scale = jnp.exp2(-SHIFT - depth)
    y_ref[0] = jnp.swapaxes(x[:, :dates] * scale, 0, 1)
    y_ref[1] = jnp.swapaxes(jnp.where(own, 0.0, imag * scale), 0, 1)


def call(kernel, shape, dtype, x):
    return pl.pallas_call(
        kernel,
        out_shape=jax.ShapeDtypeStruct(shape, dtype),
        in_specs=[VMEM],
        out_specs=VMEM,
        compiler_params=pltpu.CompilerParams(vmem_limit_bytes=32 * 1024 * 1024),
    )(x)


def on_device(slc):
    parts, dates, rows, cols = slc.shape
    blocks = lax.axis_size("date")
    pixels = LOOK_ROWS * LOOK_COLS
    count = blocks * dates
    x = slc.transpose(0, 1, 3, 2)
    x = call(split_looks, (blocks, parts * dates, pixels), jnp.bfloat16, x)
    x = lax.all_to_all(x, "date", 0, 0, tiled=True)
    x = call(pairs, (count + EXTRA, count), jnp.float32, x)
    x = lax.ppermute(x.astype(jnp.float16), ("date", "tile"), moves()).astype(jnp.float32)
    x = call(unfold, (blocks, parts * dates, count), jnp.float32, x)
    x = lax.all_to_all(x.astype(jnp.float16), "date", 0, 0, tiled=True).astype(jnp.float32)
    return call(spread, (parts, dates, blocks, count), jnp.float32, x)


def solution(mesh):
    in_specs = (P(None, "date", None, "tile"),)
    out_specs = P(None, "date", "tile", None)
    return jax.shard_map(
        on_device, mesh=mesh, in_specs=in_specs, out_specs=out_specs, check_vma=False
    )
```

```python
import jax
import jax.numpy as jnp
from jax import lax
from jax.experimental import pallas as pl
from jax.experimental.pallas import tpu as pltpu
from jax.sharding import PartitionSpec as P

LOOK_ROWS = 8
LOOK_COLS = 32
AREA = float(LOOK_ROWS * LOOK_COLS)
SHIFT = 14.0
DEEPEST = 100.0
EXTRA = 8

VMEM = pl.BlockSpec(memory_space=pltpu.VMEM)


def worked_at(look_row, half, tile):
    y = (look_row // 4 - tile // 4) % 4
    cross = (look_row // 2 % 2) ^ (tile // 2 % 2)
    return y * 8 + cross * 4 + half * 2 + ((look_row % 2) ^ (tile % 2))


def found_at(look_col, tile, h):
    source, half = look_col // 2, look_col % 2
    y = (tile // 4 - source // 4) % 4
    p = half * 2 + ((source % 2) ^ (tile % 2))
    cross = (source // 2 % 2) ^ (tile // 2 % 2)
    return y * 4 + p, cross ^ h


def moves(own):
    pairs = []
    for y in range(4):
        for z in range(16):
            h, p = z // 4 % 2, z % 4
            target = (z + (8 * h if own else 4)) % 16
            for x in range(4):
                for core in range(2):
                    here = (y * 8 + z % 8) * 16 + x * 4 + z // 8 * 2 + core
                    there = (y * 8 + target % 8) * 16 + (x + y) % 4 * 4 + target // 8 * 2 + (core ^ (p % 2))
                    pairs.append((here, there))
    return pairs


def quads():
    return [[y * 8 + h * 4 + p for y in range(4) for p in range(4)] for h in range(2)]


def exchange(x, dates):
    rows = lax.broadcasted_iota(jnp.int32, x.shape, 0)
    lanes = lax.broadcasted_iota(jnp.int32, x.shape, 1)
    height, width = x.shape
    step = dates // 2
    while step:
        low_row = (rows & step) == 0
        low_lane = (lanes & (step * LOOK_COLS)) == 0
        up = pltpu.roll(pltpu.roll(x, height - step, 0), step * LOOK_COLS, 1)
        down = pltpu.roll(pltpu.roll(x, step, 0), width - step * LOOK_COLS, 1)
        x = jnp.where(low_row == low_lane, x, jnp.where(low_row, up, down))
        step //= 2
    return x


def split_looks(x_ref, y_ref):
    parts, dates, cols, rows = x_ref.shape
    look_rows = rows // LOOK_ROWS
    tile = lax.axis_index("tile")
    for half in range(cols // LOOK_COLS):
        blocks = []
        for part in range(parts):
            block = x_ref[part, :, half * LOOK_COLS : (half + 1) * LOOK_COLS, :]
            block = block.reshape(dates * LOOK_COLS, rows).astype(jnp.float32)
            block = exchange(block.T, dates)
            blocks.append(block.reshape(look_rows, dates, dates * LOOK_COLS))
        looks = jnp.concatenate(blocks, axis=1).astype(y_ref.dtype)
        for look_row in range(look_rows):
            y_ref[worked_at(look_row, half, tile)] = looks[look_row]


def pairs(x_ref, y_ref):
    blocks, both, pixels = x_ref.shape
    dates = both // 2
    count = blocks * dates // 2
    h = lax.axis_index("date") % 8 // 4
    x = x_ref[...].astype(jnp.float32).reshape(4, 2, 4, both, pixels)
    one, turned, power_i, power_j = [], [], [], []
    dims = (((1,), (1,)), ((), ()))

    def cross(a, b):
        return lax.dot_general(a, b, dims, preferred_element_type=jnp.float32) / AREA

    i = lax.broadcasted_iota(jnp.int32, (count, count), 0)
    j = lax.broadcasted_iota(jnp.int32, (count, count), 1)
    own_real = []
    for q in range(2):
        real = x[:, q, :, :dates].reshape(count, pixels).astype(jnp.bfloat16)
        imag = x[:, q, :, dates:].reshape(count, pixels).astype(jnp.bfloat16)
        one.append(jnp.concatenate([real, imag], axis=1))
        turned.append(jnp.concatenate([imag, -real], axis=1))
        own_real.append(cross(one[q], one[q]))
        diagonal = jnp.where(i == j, own_real[q], 0.0)
        power_i.append(jnp.sum(diagonal, axis=1, keepdims=True))
        power_j.append(jnp.sum(diagonal, axis=0, keepdims=True))
    highest = jnp.max(jnp.maximum(power_j[0], power_j[1]), axis=1, keepdims=True)
    bound = highest * lax.rsqrt(highest * highest + 1e-06)
    depth = jnp.clip(jnp.floor(-jnp.log2(bound + 1e-37)), 0.0, DEEPEST)
    factor = jnp.exp2(depth + SHIFT)
    for q in range(2):
        place = q ^ h
        own = lax.rsqrt(power_i[q] * power_j[q] + 1e-06) * factor
        other = lax.rsqrt(power_i[q] * power_j[1 - q] + 1e-06) * factor
        own_imag = cross(turned[q], one[q])
        y_ref[place, :count] = jnp.where(i >= j, own_real[q], own_imag) * own
        y_ref[place, count : 2 * count] = cross(one[q], one[1 - q]) * other
        y_ref[place, 2 * count : 3 * count] = cross(turned[q], one[1 - q]) * other
        y_ref[place, 3 * count :] = jnp.broadcast_to(depth, (EXTRA, count))


def interleave(own, other, h):
    first = jnp.where(h == 0, own, other)
    second = jnp.where(h == 0, other, own)
    width = own.shape[1]
    step = width // 4
    block = lax.broadcasted_iota(jnp.int32, own.shape, 1) // step

    def by(x, blocks):
        return x if blocks == 0 else pltpu.roll(x, blocks * step % width, 1)

    def choose(a, b, c, d):
        return jnp.where(block < 2, jnp.where(block == 0, a, b), jnp.where(block == 2, c, d))

    low = choose(first, by(second, 1), by(first, 1), by(second, 2))
    high = choose(by(first, 2), by(second, 3), by(first, 3), second)
    return jnp.concatenate([low, high], axis=1)


def unfold(own_ref, other_ref, y_ref):
    peers, rows, _ = y_ref.shape
    dates = rows // 4
    count = peers * dates
    h = lax.axis_index("date") % 8 // 4
    i = lax.broadcasted_iota(jnp.int32, (count, count), 0)
    j = lax.broadcasted_iota(jnp.int32, (count, count), 1)
    for piece, x_ref in enumerate((own_ref, other_ref)):
        x = x_ref[:count]
        depth = x_ref[3 * count : 3 * count + 1]
        flipped = x.T
        real = jnp.where(i >= j, x, flipped)
        imag = jnp.where(i > j, -flipped, jnp.where(i == j, depth, x))
        real = interleave(real, x_ref[count : 2 * count], h)
        imag = interleave(imag, x_ref[2 * count : 3 * count], h)
        first = piece * 2 * dates
        y_ref[:, first : first + dates] = real.reshape(peers, dates, 2 * count)
        y_ref[:, first + dates : first + 2 * dates] = imag.reshape(peers, dates, 2 * count)


def spread(x_ref, y_ref):
    looks, both, count = x_ref.shape
    dates = both // 2
    tile, date = lax.axis_index("tile"), lax.axis_index("date")
    h = date % 8 // 4
    rows = []
    for look in range(looks):
        source, piece = found_at(look, tile, h)
        rows.append(x_ref[source * 2 + piece])
    x = jnp.stack(rows)
    shape = (looks, dates, count)
    i = lax.broadcasted_iota(jnp.int32, shape, 1)
    j = lax.broadcasted_iota(jnp.int32, shape, 2)
    own = j == i + date * dates
    imag = x[:, dates:]
    depth = jnp.sum(jnp.where(own, imag, 0.0), axis=2, keepdims=True)
    scale = jnp.exp2(-SHIFT - depth)
    y_ref[0] = jnp.swapaxes(x[:, :dates] * scale, 0, 1)
    y_ref[1] = jnp.swapaxes(jnp.where(own, 0.0, imag * scale), 0, 1)


def call(kernel, shape, dtype, *xs):
    return pl.pallas_call(
        kernel,
        out_shape=jax.ShapeDtypeStruct(shape, dtype),
        in_specs=[VMEM] * len(xs),
        out_specs=VMEM,
        compiler_params=pltpu.CompilerParams(vmem_limit_bytes=32 * 1024 * 1024),
    )(*xs)


def on_device(slc):
    parts, dates, rows, cols = slc.shape
    blocks = lax.axis_size("date")
    pixels = LOOK_ROWS * LOOK_COLS
    count = blocks * dates
    x = slc.transpose(0, 1, 3, 2)
    x = call(split_looks, (blocks, parts * dates, pixels), jnp.bfloat16, x)
    x = lax.all_to_all(x, "date", 0, 0, tiled=True)
    x = call(pairs, (2, 3 * count // 2 + EXTRA, count // 2), jnp.float32, x)
    other = lax.ppermute(x[1].astype(jnp.float16), ("date", "tile"), moves(False))
    own = lax.ppermute(x[0].astype(jnp.float16), ("date", "tile"), moves(True))
    x = call(
        unfold,
        (blocks // 2, 2 * parts * dates, count),
        jnp.float32,
        own.astype(jnp.float32),
        other.astype(jnp.float32),
    )
    x = lax.all_to_all(x.astype(jnp.float16), "date", 0, 0, axis_index_groups=quads(), tiled=True)
    x = x.astype(jnp.float32).reshape(blocks, parts * dates, count)
    return call(spread, (parts, dates, blocks, count), jnp.float32, x)


def solution(mesh):
    in_specs = (P(None, "date", None, "tile"),)
    out_specs = P(None, "date", "tile", None)
    return jax.shard_map(
        on_device, mesh=mesh, in_specs=in_specs, out_specs=out_specs, check_vma=False
    )
```

```python
import jax
import jax.numpy as jnp
from jax import lax
from jax.experimental import pallas as pl
from jax.experimental.pallas import tpu as pltpu
from jax.sharding import PartitionSpec as P

LOOK_ROWS = 8
LOOK_COLS = 32
AREA = float(LOOK_ROWS * LOOK_COLS)
SHIFT = 14.0
DEEPEST = 100.0
EXTRA = 8

VMEM = pl.BlockSpec(memory_space=pltpu.VMEM)


def worked_at(look_row, half, tile):
    y = (look_row // 4 - tile // 4) % 4
    cross = (look_row // 2 % 2) ^ (tile // 2 % 2)
    return y * 8 + cross * 4 + half * 2 + ((look_row % 2) ^ (tile % 2))


def found_at(look_col, tile, h):
    source, half = look_col // 2, look_col % 2
    y = (tile // 4 - source // 4) % 4
    p = half * 2 + ((source % 2) ^ (tile % 2))
    cross = (source // 2 % 2) ^ (tile // 2 % 2)
    return y * 4 + p, cross ^ h


def moves(own):
    pairs = []
    for y in range(4):
        for z in range(16):
            h, p = z // 4 % 2, z % 4
            target = (z + (8 * h if own else 4)) % 16
            for x in range(4):
                for core in range(2):
                    here = (y * 8 + z % 8) * 16 + x * 4 + z // 8 * 2 + core
                    there = (y * 8 + target % 8) * 16 + (x + y) % 4 * 4 + target // 8 * 2 + (core ^ (p % 2))
                    pairs.append((here, there))
    return pairs


def quads():
    return [[y * 8 + h * 4 + p for y in range(4) for p in range(4)] for h in range(2)]


def exchange(x):
    width = x.shape[2] // 2
    low, high = x[:, :, :width], x[:, :, width:]
    row = lax.broadcasted_iota(jnp.int32, low.shape, 1)
    lane = lax.broadcasted_iota(jnp.int32, low.shape, 2) // LOOK_COLS
    low, high = (
        jnp.where(row < 4, low, pltpu.roll(high, 4, 1)),
        jnp.where(row < 4, pltpu.roll(low, 4, 1), high),
    )

    def swap(x, bit):
        step = bit * LOOK_COLS
        up = pltpu.roll(pltpu.roll(x, LOOK_ROWS - bit, 1), step, 2)
        down = pltpu.roll(pltpu.roll(x, bit, 1), width - step, 2)
        low_row = (row & bit) == 0
        return jnp.where(low_row == ((lane & bit) == 0), x, jnp.where(low_row, up, down))

    return jnp.concatenate([swap(swap(low, 2), 1), swap(swap(high, 2), 1)], axis=2)


def split_looks(x_ref, y_ref):
    parts, dates, cols, rows = x_ref.shape
    look_rows = rows // LOOK_ROWS
    tile = lax.axis_index("tile")
    for half in range(cols // LOOK_COLS):
        blocks = []
        for part in range(parts):
            block = x_ref[part, :, half * LOOK_COLS : (half + 1) * LOOK_COLS, :]
            block = block.reshape(dates * LOOK_COLS, rows).astype(jnp.float32)
            blocks.append(exchange(block.T.reshape(look_rows, LOOK_ROWS, dates * LOOK_COLS)))
        looks = jnp.concatenate(blocks, axis=1).astype(y_ref.dtype)
        for look_row in range(look_rows):
            y_ref[worked_at(look_row, half, tile)] = looks[look_row]


def pairs(x_ref, own_ref, other_ref):
    blocks, both, pixels = x_ref.shape
    dates = both // 2
    count = blocks * dates // 2
    h = lax.axis_index("date") % 8 // 4
    x = x_ref[...].astype(jnp.float32).reshape(4, 2, 4, both, pixels)
    one, turned, power_i, power_j = [], [], [], []
    dims = (((1,), (1,)), ((), ()))

    def cross(a, b):
        return lax.dot_general(a, b, dims, preferred_element_type=jnp.float32) / AREA

    i = lax.broadcasted_iota(jnp.int32, (count, count), 0)
    j = lax.broadcasted_iota(jnp.int32, (count, count), 1)
    own_real = []
    for q in range(2):
        real = x[:, q, :, :dates].reshape(count, pixels).astype(jnp.bfloat16)
        imag = x[:, q, :, dates:].reshape(count, pixels).astype(jnp.bfloat16)
        one.append(jnp.concatenate([real, imag], axis=1))
        turned.append(jnp.concatenate([imag, -real], axis=1))
        own_real.append(cross(one[q], one[q]))
        diagonal = jnp.where(i == j, own_real[q], 0.0)
        power_i.append(jnp.sum(diagonal, axis=1, keepdims=True))
        power_j.append(jnp.sum(diagonal, axis=0, keepdims=True))
    highest = jnp.max(jnp.maximum(power_j[0], power_j[1]), axis=1, keepdims=True)
    bound = highest * lax.rsqrt(highest * highest + 1e-06)
    depth = jnp.clip(jnp.floor(-jnp.log2(bound + 1e-37)), 0.0, DEEPEST)
    factor = jnp.exp2(depth + SHIFT)
    pieces = []
    for q in range(2):
        own = lax.rsqrt(power_i[q] * power_j[q] + 1e-06) * factor
        other = lax.rsqrt(power_i[q] * power_j[1 - q] + 1e-06) * factor
        pieces.append(
            (
                jnp.where(i >= j, own_real[q], cross(turned[q], one[q])) * own,
                cross(one[q], one[1 - q]) * other,
                cross(turned[q], one[1 - q]) * other,
            )
        )
    for block, (first, second) in enumerate(zip(*pieces)):
        rows = slice(block * count, (block + 1) * count)
        own_ref[rows] = jnp.where(h == 0, first, second)
        other_ref[rows] = jnp.where(h == 0, second, first)
    for y_ref in (own_ref, other_ref):
        y_ref[3 * count :] = jnp.broadcast_to(depth, (EXTRA, count))


def interleave(own, other, h):
    first = jnp.where(h == 0, own, other)
    second = jnp.where(h == 0, other, own)
    width = own.shape[1]
    step = width // 4
    block = lax.broadcasted_iota(jnp.int32, own.shape, 1) // step

    def by(x, blocks):
        return x if blocks == 0 else pltpu.roll(x, blocks * step % width, 1)

    def choose(a, b, c, d):
        return jnp.where(block < 2, jnp.where(block == 0, a, b), jnp.where(block == 2, c, d))

    low = choose(first, by(second, 1), by(first, 1), by(second, 2))
    high = choose(by(first, 2), by(second, 3), by(first, 3), second)
    return jnp.concatenate([low, high], axis=1)


def unfold(own_ref, other_ref, y_ref):
    peers, rows, _ = y_ref.shape
    dates = rows // 4
    count = peers * dates
    h = lax.axis_index("date") % 8 // 4
    i = lax.broadcasted_iota(jnp.int32, (count, count), 0)
    j = lax.broadcasted_iota(jnp.int32, (count, count), 1)
    for piece, x_ref in enumerate((own_ref, other_ref)):
        x = x_ref[:count]
        depth = x_ref[3 * count : 3 * count + 1]
        flipped = x.T
        real = jnp.where(i >= j, x, flipped)
        imag = jnp.where(i > j, -flipped, jnp.where(i == j, depth, x))
        real = interleave(real, x_ref[count : 2 * count], h)
        imag = interleave(imag, x_ref[2 * count : 3 * count], h)
        first = piece * 2 * dates
        y_ref[:, first : first + dates] = real.reshape(peers, dates, 2 * count)
        y_ref[:, first + dates : first + 2 * dates] = imag.reshape(peers, dates, 2 * count)


def spread(x_ref, y_ref):
    looks, both, count = x_ref.shape
    dates = both // 2
    tile, date = lax.axis_index("tile"), lax.axis_index("date")
    h = date % 8 // 4
    rows = []
    for look in range(looks):
        source, piece = found_at(look, tile, h)
        rows.append(x_ref[source * 2 + piece])
    x = jnp.stack(rows)
    shape = (looks, dates, count)
    i = lax.broadcasted_iota(jnp.int32, shape, 1)
    j = lax.broadcasted_iota(jnp.int32, shape, 2)
    own = j == i + date * dates
    imag = x[:, dates:]
    depth = jnp.sum(jnp.where(own, imag, 0.0), axis=2, keepdims=True)
    scale = jnp.exp2(-SHIFT - depth)
    y_ref[0] = jnp.swapaxes(x[:, :dates] * scale, 0, 1)
    y_ref[1] = jnp.swapaxes(jnp.where(own, 0.0, imag * scale), 0, 1)


def call(kernel, out_shape, *xs):
    return pl.pallas_call(
        kernel,
        out_shape=out_shape,
        in_specs=[VMEM] * len(xs),
        out_specs=jax.tree.map(lambda _: VMEM, out_shape),
        compiler_params=pltpu.CompilerParams(vmem_limit_bytes=32 * 1024 * 1024),
    )(*xs)


def on_device(slc):
    parts, dates, rows, cols = slc.shape
    blocks = lax.axis_size("date")
    pixels = LOOK_ROWS * LOOK_COLS
    count = blocks * dates
    x = slc.transpose(0, 1, 3, 2)
    x = call(split_looks, jax.ShapeDtypeStruct((blocks, parts * dates, pixels), jnp.bfloat16), x)
    x = lax.all_to_all(x, "date", 0, 0, tiled=True)
    shape = jax.ShapeDtypeStruct((3 * count // 2 + EXTRA, count // 2), jnp.float32)
    own, other = call(pairs, (shape, shape), x)
    other = lax.ppermute(other.astype(jnp.float16), ("date", "tile"), moves(False))
    own = lax.ppermute(own.astype(jnp.float16), ("date", "tile"), moves(True))
    x = call(
        unfold,
        jax.ShapeDtypeStruct((blocks // 2, 2 * parts * dates, count), jnp.float32),
        own.astype(jnp.float32),
        other.astype(jnp.float32),
    )
    x = lax.all_to_all(x.astype(jnp.float16), "date", 0, 0, axis_index_groups=quads(), tiled=True)
    x = x.astype(jnp.float32).reshape(blocks, parts * dates, count)
    return call(spread, jax.ShapeDtypeStruct((parts, dates, blocks, count), jnp.float32), x)


def solution(mesh):
    in_specs = (P(None, "date", None, "tile"),)
    out_specs = P(None, "date", "tile", None)
    return jax.shard_map(
        on_device, mesh=mesh, in_specs=in_specs, out_specs=out_specs, check_vma=False
    )
```

```python
import jax
import jax.numpy as jnp
from jax import lax
from jax.experimental import pallas as pl
from jax.experimental.pallas import tpu as pltpu
from jax.sharding import PartitionSpec as P

LOOK_ROWS = 8
LOOK_COLS = 32
AREA = float(LOOK_ROWS * LOOK_COLS)
SHIFT = 14.0
DEEPEST = 100.0
EXTRA = 8

VMEM = pl.BlockSpec(memory_space=pltpu.VMEM)


def worked_at(look_row, half, tile):
    y = (look_row // 4 - tile // 4) % 4
    cross = (look_row // 2 % 2) ^ (tile // 2 % 2)
    return y * 8 + cross * 4 + half * 2 + ((look_row % 2) ^ (tile % 2))


def found_at(look_col, tile, h):
    source, half = look_col // 2, look_col % 2
    y = (tile // 4 - source // 4) % 4
    p = half * 2 + ((source % 2) ^ (tile % 2))
    cross = (source // 2 % 2) ^ (tile // 2 % 2)
    return 15 - (y * 4 + p), cross ^ h


def moves(own):
    pairs = []
    for y in range(4):
        for z in range(16):
            h, p = z // 4 % 2, z % 4
            target = (z + (8 * h if own else 4)) % 16
            for x in range(4):
                for core in range(2):
                    here = (y * 8 + z % 8) * 16 + x * 4 + z // 8 * 2 + core
                    there = (y * 8 + target % 8) * 16 + (x + y) % 4 * 4 + target // 8 * 2 + (core ^ (p % 2))
                    pairs.append((here, there))
    return pairs


def quads():
    return [[y * 8 + h * 4 + p for y in range(3, -1, -1) for p in range(3, -1, -1)] for h in range(2)]


def exchange(x):
    width = x.shape[2] // 2
    low, high = x[:, :, :width], x[:, :, width:]
    row = lax.broadcasted_iota(jnp.int32, low.shape, 1)
    lane = lax.broadcasted_iota(jnp.int32, low.shape, 2) // LOOK_COLS
    low, high = (
        jnp.where(row < 4, low, pltpu.roll(high, 4, 1)),
        jnp.where(row < 4, pltpu.roll(low, 4, 1), high),
    )

    def swap(x, bit):
        step = bit * LOOK_COLS
        up = pltpu.roll(pltpu.roll(x, LOOK_ROWS - bit, 1), step, 2)
        down = pltpu.roll(pltpu.roll(x, bit, 1), width - step, 2)
        low_row = (row & bit) == 0
        return jnp.where(low_row == ((lane & bit) == 0), x, jnp.where(low_row, up, down))

    return jnp.concatenate([swap(swap(low, 2), 1), swap(swap(high, 2), 1)], axis=2)


def split_looks(x_ref, y_ref):
    parts, dates, cols, rows = x_ref.shape
    look_rows = rows // LOOK_ROWS
    tile = lax.axis_index("tile")
    for half in range(cols // LOOK_COLS):
        blocks = []
        for part in range(parts):
            block = x_ref[part, :, half * LOOK_COLS : (half + 1) * LOOK_COLS, :]
            block = block.reshape(dates * LOOK_COLS, rows).astype(jnp.float32)
            blocks.append(exchange(block.T.reshape(look_rows, LOOK_ROWS, dates * LOOK_COLS)))
        looks = jnp.concatenate(blocks, axis=1).astype(y_ref.dtype)
        for look_row in range(look_rows):
            y_ref[worked_at(look_row, half, tile)] = looks[look_row]


def pairs(x_ref, own_ref, other_ref):
    blocks, both, pixels = x_ref.shape
    dates = both // 2
    count = blocks * dates // 2
    h = lax.axis_index("date") % 8 // 4
    x = x_ref[...].astype(jnp.float32).reshape(4, 2, 4, both, pixels)
    one, turned, power_i, power_j = [], [], [], []
    dims = (((1,), (1,)), ((), ()))

    def cross(a, b):
        return lax.dot_general(a, b, dims, preferred_element_type=jnp.float32) / AREA

    i = lax.broadcasted_iota(jnp.int32, (count, count), 0)
    j = lax.broadcasted_iota(jnp.int32, (count, count), 1)
    own_real = []
    for q in range(2):
        real = x[:, q, :, :dates].reshape(count, pixels).astype(jnp.bfloat16)
        imag = x[:, q, :, dates:].reshape(count, pixels).astype(jnp.bfloat16)
        one.append(jnp.concatenate([real, imag], axis=1))
        turned.append(jnp.concatenate([imag, -real], axis=1))
        own_real.append(cross(one[q], one[q]))
        diagonal = jnp.where(i == j, own_real[q], 0.0)
        power_i.append(jnp.sum(diagonal, axis=1, keepdims=True))
        power_j.append(jnp.sum(diagonal, axis=0, keepdims=True))
    highest = jnp.max(jnp.maximum(power_j[0], power_j[1]), axis=1, keepdims=True)
    bound = highest * lax.rsqrt(highest * highest + 1e-06)
    depth = jnp.clip(jnp.floor(-jnp.log2(bound + 1e-37)), 0.0, DEEPEST)
    factor = jnp.exp2(depth + SHIFT)
    pieces = []
    for q in range(2):
        own = lax.rsqrt(power_i[q] * power_j[q] + 1e-06) * factor
        other = lax.rsqrt(power_i[q] * power_j[1 - q] + 1e-06) * factor
        pieces.append(
            (
                jnp.where(i >= j, own_real[q], cross(turned[q], one[q])) * own,
                cross(one[q], one[1 - q]) * other,
                cross(turned[q], one[1 - q]) * other,
            )
        )
    for block, (first, second) in enumerate(zip(*pieces)):
        rows = slice(block * count, (block + 1) * count)
        own_ref[rows] = jnp.where(h == 0, first, second)
        other_ref[rows] = jnp.where(h == 0, second, first)
    for y_ref in (own_ref, other_ref):
        y_ref[3 * count :] = jnp.broadcast_to(depth, (EXTRA, count))


def interleave(own, other, h):
    first = jnp.where(h == 0, own, other)
    second = jnp.where(h == 0, other, own)
    width = own.shape[1]
    step = width // 4
    block = lax.broadcasted_iota(jnp.int32, own.shape, 1) // step

    def by(x, blocks):
        return x if blocks == 0 else pltpu.roll(x, blocks * step % width, 1)

    def choose(a, b, c, d):
        return jnp.where(block < 2, jnp.where(block == 0, a, b), jnp.where(block == 2, c, d))

    low = choose(first, by(second, 1), by(first, 1), by(second, 2))
    high = choose(by(first, 2), by(second, 3), by(first, 3), second)
    return jnp.concatenate([low, high], axis=1)


def unfold(own_ref, other_ref, y_ref):
    peers, rows, _ = y_ref.shape
    dates = rows // 4
    count = peers * dates
    h = lax.axis_index("date") % 8 // 4
    i = lax.broadcasted_iota(jnp.int32, (count, count), 0)
    j = lax.broadcasted_iota(jnp.int32, (count, count), 1)
    for piece, x_ref in enumerate((own_ref, other_ref)):
        x = x_ref[:count]
        depth = x_ref[3 * count : 3 * count + 1]
        flipped = x.T
        real = jnp.where(i >= j, x, flipped)
        imag = jnp.where(i > j, -flipped, jnp.where(i == j, depth, x))
        real = interleave(real, x_ref[count : 2 * count], h)
        imag = interleave(imag, x_ref[2 * count : 3 * count], h)
        first = piece * 2 * dates
        real = real.reshape(peers, dates, 2 * count)
        imag = imag.reshape(peers, dates, 2 * count)
        for peer in range(peers):
            y_ref[peers - 1 - peer, first : first + dates] = real[peer]
            y_ref[peers - 1 - peer, first + dates : first + 2 * dates] = imag[peer]


def spread(x_ref, y_ref):
    looks, both, count = x_ref.shape
    dates = both // 2
    tile, date = lax.axis_index("tile"), lax.axis_index("date")
    h = date % 8 // 4
    rows = []
    for look in range(looks):
        source, piece = found_at(look, tile, h)
        rows.append(x_ref[source * 2 + piece])
    x = jnp.stack(rows)
    shape = (looks, dates, count)
    i = lax.broadcasted_iota(jnp.int32, shape, 1)
    j = lax.broadcasted_iota(jnp.int32, shape, 2)
    own = j == i + date * dates
    imag = x[:, dates:]
    depth = jnp.sum(jnp.where(own, imag, 0.0), axis=2, keepdims=True)
    scale = jnp.exp2(-SHIFT - depth)
    y_ref[0] = jnp.swapaxes(x[:, :dates] * scale, 0, 1)
    y_ref[1] = jnp.swapaxes(jnp.where(own, 0.0, imag * scale), 0, 1)


def call(kernel, out_shape, *xs):
    return pl.pallas_call(
        kernel,
        out_shape=out_shape,
        in_specs=[VMEM] * len(xs),
        out_specs=jax.tree.map(lambda _: VMEM, out_shape),
        compiler_params=pltpu.CompilerParams(vmem_limit_bytes=32 * 1024 * 1024),
    )(*xs)


def on_device(slc):
    parts, dates, rows, cols = slc.shape
    blocks = lax.axis_size("date")
    pixels = LOOK_ROWS * LOOK_COLS
    count = blocks * dates
    x = slc.transpose(0, 1, 3, 2)
    x = call(split_looks, jax.ShapeDtypeStruct((blocks, parts * dates, pixels), jnp.bfloat16), x)
    x = lax.all_to_all(x, "date", 0, 0, tiled=True)
    shape = jax.ShapeDtypeStruct((3 * count // 2 + EXTRA, count // 2), jnp.float32)
    own, other = call(pairs, (shape, shape), x)
    other = lax.ppermute(other.astype(jnp.float16), ("date", "tile"), moves(False))
    own = lax.ppermute(own.astype(jnp.float16), ("date", "tile"), moves(True))
    x = call(
        unfold,
        jax.ShapeDtypeStruct((blocks // 2, 2 * parts * dates, count), jnp.float32),
        own.astype(jnp.float32),
        other.astype(jnp.float32),
    )
    x = lax.all_to_all(x.astype(jnp.float16), "date", 0, 0, axis_index_groups=quads(), tiled=True)
    x = x.astype(jnp.float32).reshape(blocks, parts * dates, count)
    return call(spread, jax.ShapeDtypeStruct((parts, dates, blocks, count), jnp.float32), x)


def solution(mesh):
    in_specs = (P(None, "date", None, "tile"),)
    out_specs = P(None, "date", "tile", None)
    return jax.shard_map(
        on_device, mesh=mesh, in_specs=in_specs, out_specs=out_specs, check_vma=False
    )
```

```python
import jax
import jax.numpy as jnp
from jax import lax
from jax.experimental import pallas as pl
from jax.experimental.pallas import tpu as pltpu
from jax.sharding import PartitionSpec as P

LOOK_ROWS = 8
LOOK_COLS = 32
AREA = float(LOOK_ROWS * LOOK_COLS)
SHIFT = 14.0
DEEPEST = 100.0
EXTRA = 8

VMEM = pl.BlockSpec(memory_space=pltpu.VMEM)


def order(y, z_lo):
    return 31 - (jnp.where(z_lo < 4, 2 * z_lo, 15 - 2 * z_lo) * 4 + y)


def middle_first():
    return [y * 8 + z_lo for z_lo in (4, 3, 5, 2, 6, 1, 7, 0) for y in (3, 2, 1, 0)]


def worked_at(look_row, half, tile):
    y = (look_row // 4 - tile // 4) % 4
    cross = (look_row // 2 % 2) ^ (tile // 2 % 2)
    return order(y, cross * 4 + half * 2 + ((look_row % 2) ^ (tile % 2)))


def found_at(look_col, tile, h):
    source, half = look_col // 2, look_col % 2
    y = (tile // 4 - source // 4) % 4
    p = half * 2 + ((source % 2) ^ (tile % 2))
    cross = (source // 2 % 2) ^ (tile // 2 % 2)
    turn = jnp.where(p == 2, 0, jnp.where(p == 1, 1, jnp.where(p == 3, 2, 3)))
    return (3 - y) * 4 + turn, cross ^ h


def moves(own):
    pairs = []
    for y in range(4):
        for z in range(16):
            h, p = z // 4 % 2, z % 4
            target = (z + (8 * h if own else 4)) % 16
            for x in range(4):
                for core in range(2):
                    here = (y * 8 + z % 8) * 16 + x * 4 + z // 8 * 2 + core
                    there = (y * 8 + target % 8) * 16 + (x + y) % 4 * 4 + target // 8 * 2 + (core ^ (p % 2))
                    pairs.append((here, there))
    return pairs


SEATS = [y * 4 + p for y in (3, 2, 1, 0) for p in (2, 1, 3, 0)]


def quads():
    return [[seat // 4 * 8 + h * 4 + seat % 4 for seat in SEATS] for h in range(2)]


def exchange(x):
    width = x.shape[2] // 2
    low, high = x[:, :, :width], x[:, :, width:]
    row = lax.broadcasted_iota(jnp.int32, low.shape, 1)
    lane = lax.broadcasted_iota(jnp.int32, low.shape, 2) // LOOK_COLS
    low, high = (
        jnp.where(row < 4, low, pltpu.roll(high, 4, 1)),
        jnp.where(row < 4, pltpu.roll(low, 4, 1), high),
    )

    def swap(x, bit):
        step = bit * LOOK_COLS
        up = pltpu.roll(pltpu.roll(x, LOOK_ROWS - bit, 1), step, 2)
        down = pltpu.roll(pltpu.roll(x, bit, 1), width - step, 2)
        low_row = (row & bit) == 0
        return jnp.where(low_row == ((lane & bit) == 0), x, jnp.where(low_row, up, down))

    return jnp.concatenate([swap(swap(low, 2), 1), swap(swap(high, 2), 1)], axis=2)


def split_looks(x_ref, y_ref):
    parts, dates, cols, rows = x_ref.shape
    look_rows = rows // LOOK_ROWS
    tile = lax.axis_index("tile")
    for half in range(cols // LOOK_COLS):
        blocks = []
        for part in range(parts):
            block = x_ref[part, :, half * LOOK_COLS : (half + 1) * LOOK_COLS, :]
            block = block.reshape(dates * LOOK_COLS, rows).astype(jnp.float32)
            blocks.append(exchange(block.T.reshape(look_rows, LOOK_ROWS, dates * LOOK_COLS)))
        looks = jnp.concatenate(blocks, axis=1).astype(y_ref.dtype)
        for look_row in range(look_rows):
            y_ref[worked_at(look_row, half, tile)] = looks[look_row]


def pairs(x_ref, own_ref, other_ref):
    blocks, both, pixels = x_ref.shape
    dates = both // 2
    count = blocks * dates // 2
    h = lax.axis_index("date") % 8 // 4
    places = [middle_first().index(date) for date in range(blocks)]
    x = jnp.stack([x_ref[place] for place in places]).astype(jnp.float32).reshape(4, 2, 4, both, pixels)
    one, turned, power_i, power_j = [], [], [], []
    dims = (((1,), (1,)), ((), ()))

    def cross(a, b):
        return lax.dot_general(a, b, dims, preferred_element_type=jnp.float32) / AREA

    i = lax.broadcasted_iota(jnp.int32, (count, count), 0)
    j = lax.broadcasted_iota(jnp.int32, (count, count), 1)
    own_real = []
    for q in range(2):
        real = x[:, q, :, :dates].reshape(count, pixels).astype(jnp.bfloat16)
        imag = x[:, q, :, dates:].reshape(count, pixels).astype(jnp.bfloat16)
        one.append(jnp.concatenate([real, imag], axis=1))
        turned.append(jnp.concatenate([imag, -real], axis=1))
        own_real.append(cross(one[q], one[q]))
        diagonal = jnp.where(i == j, own_real[q], 0.0)
        power_i.append(jnp.sum(diagonal, axis=1, keepdims=True))
        power_j.append(jnp.sum(diagonal, axis=0, keepdims=True))
    highest = jnp.max(jnp.maximum(power_j[0], power_j[1]), axis=1, keepdims=True)
    bound = highest * lax.rsqrt(highest * highest + 1e-06)
    depth = jnp.clip(jnp.floor(-jnp.log2(bound + 1e-37)), 0.0, DEEPEST)
    factor = jnp.exp2(depth + SHIFT)
    pieces = []
    for q in range(2):
        own = lax.rsqrt(power_i[q] * power_j[q] + 1e-06) * factor
        other = lax.rsqrt(power_i[q] * power_j[1 - q] + 1e-06) * factor
        pieces.append(
            (
                jnp.where(i >= j, own_real[q], cross(turned[q], one[q])) * own,
                cross(one[q], one[1 - q]) * other,
                cross(turned[q], one[1 - q]) * other,
            )
        )
    for block, (first, second) in enumerate(zip(*pieces)):
        rows = slice(block * count, (block + 1) * count)
        own_ref[rows] = jnp.where(h == 0, first, second)
        other_ref[rows] = jnp.where(h == 0, second, first)
    for y_ref in (own_ref, other_ref):
        y_ref[3 * count :] = jnp.broadcast_to(depth, (EXTRA, count))


def interleave(own, other, h):
    first = jnp.where(h == 0, own, other)
    second = jnp.where(h == 0, other, own)
    width = own.shape[1]
    step = width // 4
    block = lax.broadcasted_iota(jnp.int32, own.shape, 1) // step

    def by(x, blocks):
        return x if blocks == 0 else pltpu.roll(x, blocks * step % width, 1)

    def choose(a, b, c, d):
        return jnp.where(block < 2, jnp.where(block == 0, a, b), jnp.where(block == 2, c, d))

    low = choose(first, by(second, 1), by(first, 1), by(second, 2))
    high = choose(by(first, 2), by(second, 3), by(first, 3), second)
    return jnp.concatenate([low, high], axis=1)


def unfold(own_ref, other_ref, y_ref):
    peers, rows, _ = y_ref.shape
    dates = rows // 4
    count = peers * dates
    h = lax.axis_index("date") % 8 // 4
    i = lax.broadcasted_iota(jnp.int32, (count, count), 0)
    j = lax.broadcasted_iota(jnp.int32, (count, count), 1)
    for piece, x_ref in enumerate((own_ref, other_ref)):
        x = x_ref[:count]
        depth = x_ref[3 * count : 3 * count + 1]
        flipped = x.T
        real = jnp.where(i >= j, x, flipped)
        imag = jnp.where(i > j, -flipped, jnp.where(i == j, depth, x))
        real = interleave(real, x_ref[count : 2 * count], h)
        imag = interleave(imag, x_ref[2 * count : 3 * count], h)
        first = piece * 2 * dates
        real = real.reshape(peers, dates, 2 * count)
        imag = imag.reshape(peers, dates, 2 * count)
        for place, peer in enumerate(SEATS):
            y_ref[place, first : first + dates] = real[peer]
            y_ref[place, first + dates : first + 2 * dates] = imag[peer]


def spread(x_ref, y_ref):
    looks, both, count = x_ref.shape
    dates = both // 2
    tile, date = lax.axis_index("tile"), lax.axis_index("date")
    h = date % 8 // 4
    rows = []
    for look in range(looks):
        source, piece = found_at(look, tile, h)
        rows.append(x_ref[source * 2 + piece])
    x = jnp.stack(rows)
    shape = (looks, dates, count)
    i = lax.broadcasted_iota(jnp.int32, shape, 1)
    j = lax.broadcasted_iota(jnp.int32, shape, 2)
    own = j == i + date * dates
    imag = x[:, dates:]
    depth = jnp.sum(jnp.where(own, imag, 0.0), axis=2, keepdims=True)
    scale = jnp.exp2(-SHIFT - depth)
    y_ref[0] = jnp.swapaxes(x[:, :dates] * scale, 0, 1)
    y_ref[1] = jnp.swapaxes(jnp.where(own, 0.0, imag * scale), 0, 1)


def call(kernel, out_shape, *xs):
    return pl.pallas_call(
        kernel,
        out_shape=out_shape,
        in_specs=[VMEM] * len(xs),
        out_specs=jax.tree.map(lambda _: VMEM, out_shape),
        compiler_params=pltpu.CompilerParams(vmem_limit_bytes=32 * 1024 * 1024),
    )(*xs)


def on_device(slc):
    parts, dates, rows, cols = slc.shape
    blocks = lax.axis_size("date")
    pixels = LOOK_ROWS * LOOK_COLS
    count = blocks * dates
    x = slc.transpose(0, 1, 3, 2)
    x = call(split_looks, jax.ShapeDtypeStruct((blocks, parts * dates, pixels), jnp.bfloat16), x)
    x = lax.all_to_all(x, "date", 0, 0, axis_index_groups=[middle_first()], tiled=True)
    shape = jax.ShapeDtypeStruct((3 * count // 2 + EXTRA, count // 2), jnp.float32)
    own, other = call(pairs, (shape, shape), x)
    other = lax.ppermute(other.astype(jnp.float16), ("date", "tile"), moves(False))
    own = lax.ppermute(own.astype(jnp.float16), ("date", "tile"), moves(True))
    x = call(
        unfold,
        jax.ShapeDtypeStruct((blocks // 2, 2 * parts * dates, count), jnp.float32),
        own.astype(jnp.float32),
        other.astype(jnp.float32),
    )
    x = lax.all_to_all(x.astype(jnp.float16), "date", 0, 0, axis_index_groups=quads(), tiled=True)
    x = x.astype(jnp.float32).reshape(blocks, parts * dates, count)
    return call(spread, jax.ShapeDtypeStruct((parts, dates, blocks, count), jnp.float32), x)


def solution(mesh):
    in_specs = (P(None, "date", None, "tile"),)
    out_specs = P(None, "date", "tile", None)
    return jax.shard_map(
        on_device, mesh=mesh, in_specs=in_specs, out_specs=out_specs, check_vma=False
    )
```

```python
import jax
import jax.numpy as jnp
from jax import lax
from jax.experimental import pallas as pl
from jax.experimental.pallas import tpu as pltpu
from jax.sharding import PartitionSpec as P

LOOK_ROWS = 8
LOOK_COLS = 32
AREA = float(LOOK_ROWS * LOOK_COLS)
SHIFT = 14.0
DEEPEST = 100.0
EXTRA = 8

VMEM = pl.BlockSpec(memory_space=pltpu.VMEM)


def order(y, z_lo):
    return 31 - (jnp.where(z_lo < 4, 2 * z_lo, 15 - 2 * z_lo) * 4 + y)


def middle_first():
    return [y * 8 + z_lo for z_lo in (4, 3, 5, 2, 6, 1, 7, 0) for y in (3, 2, 1, 0)]


def worked_at(look_row, half, tile):
    y = (look_row // 4 - tile // 4) % 4
    cross = (look_row // 2 % 2) ^ (tile // 2 % 2)
    return order(y, cross * 4 + half * 2 + ((look_row % 2) ^ (tile % 2)))


def found_at(look_col, tile, h):
    source, half = look_col // 2, look_col % 2
    y = (tile // 4 - source // 4) % 4
    p = half * 2 + ((source % 2) ^ (tile % 2))
    cross = (source // 2 % 2) ^ (tile // 2 % 2)
    turn = jnp.where(p == 2, 0, jnp.where(p == 1, 1, jnp.where(p == 3, 2, 3)))
    return turn * 4 + 3 - y, cross ^ h


def moves(own):
    pairs = []
    for y in range(4):
        for z in range(16):
            h, p = z // 4 % 2, z % 4
            target = (z + (8 * h if own else 4)) % 16
            for x in range(4):
                for core in range(2):
                    here = (y * 8 + z % 8) * 16 + x * 4 + z // 8 * 2 + core
                    there = (y * 8 + target % 8) * 16 + (x + y) % 4 * 4 + target // 8 * 2 + (core ^ (p % 2))
                    pairs.append((here, there))
    return pairs


SEATS = [y * 4 + p for p in (2, 1, 3, 0) for y in (3, 2, 1, 0)]


def quads():
    return [[seat // 4 * 8 + h * 4 + seat % 4 for seat in SEATS] for h in range(2)]


def exchange(x):
    width = x.shape[2] // 2
    low, high = x[:, :, :width], x[:, :, width:]
    row = lax.broadcasted_iota(jnp.int32, low.shape, 1)
    lane = lax.broadcasted_iota(jnp.int32, low.shape, 2) // LOOK_COLS
    low, high = (
        jnp.where(row < 4, low, pltpu.roll(high, 4, 1)),
        jnp.where(row < 4, pltpu.roll(low, 4, 1), high),
    )

    def swap(x, bit):
        step = bit * LOOK_COLS
        up = pltpu.roll(pltpu.roll(x, LOOK_ROWS - bit, 1), step, 2)
        down = pltpu.roll(pltpu.roll(x, bit, 1), width - step, 2)
        low_row = (row & bit) == 0
        return jnp.where(low_row == ((lane & bit) == 0), x, jnp.where(low_row, up, down))

    return jnp.concatenate([swap(swap(low, 2), 1), swap(swap(high, 2), 1)], axis=2)


def split_looks(x_ref, y_ref):
    parts, dates, cols, rows = x_ref.shape
    look_rows = rows // LOOK_ROWS
    tile = lax.axis_index("tile")
    for half in range(cols // LOOK_COLS):
        blocks = []
        for part in range(parts):
            block = x_ref[part, :, half * LOOK_COLS : (half + 1) * LOOK_COLS, :]
            block = block.reshape(dates * LOOK_COLS, rows).astype(jnp.float32)
            blocks.append(exchange(block.T.reshape(look_rows, LOOK_ROWS, dates * LOOK_COLS)))
        looks = jnp.concatenate(blocks, axis=1).astype(y_ref.dtype)
        for look_row in range(look_rows):
            y_ref[worked_at(look_row, half, tile)] = looks[look_row]


def pairs(x_ref, own_ref, other_ref):
    blocks, both, pixels = x_ref.shape
    dates = both // 2
    count = blocks * dates // 2
    h = lax.axis_index("date") % 8 // 4
    places = [middle_first().index(date) for date in range(blocks)]
    x = jnp.stack([x_ref[place] for place in places]).astype(jnp.float32).reshape(4, 2, 4, both, pixels)
    one, turned, power_i, power_j = [], [], [], []
    dims = (((1,), (1,)), ((), ()))

    def cross(a, b):
        return lax.dot_general(a, b, dims, preferred_element_type=jnp.float32) / AREA

    i = lax.broadcasted_iota(jnp.int32, (count, count), 0)
    j = lax.broadcasted_iota(jnp.int32, (count, count), 1)
    own_real = []
    for q in range(2):
        real = x[:, q, :, :dates].reshape(count, pixels).astype(jnp.bfloat16)
        imag = x[:, q, :, dates:].reshape(count, pixels).astype(jnp.bfloat16)
        one.append(jnp.concatenate([real, imag], axis=1))
        turned.append(jnp.concatenate([imag, -real], axis=1))
        own_real.append(cross(one[q], one[q]))
        diagonal = jnp.where(i == j, own_real[q], 0.0)
        power_i.append(jnp.sum(diagonal, axis=1, keepdims=True))
        power_j.append(jnp.sum(diagonal, axis=0, keepdims=True))
    highest = jnp.max(jnp.maximum(power_j[0], power_j[1]), axis=1, keepdims=True)
    bound = highest * lax.rsqrt(highest * highest + 1e-06)
    depth = jnp.clip(jnp.floor(-jnp.log2(bound + 1e-37)), 0.0, DEEPEST)
    factor = jnp.exp2(depth + SHIFT)
    pieces = []
    for q in range(2):
        own = lax.rsqrt(power_i[q] * power_j[q] + 1e-06) * factor
        other = lax.rsqrt(power_i[q] * power_j[1 - q] + 1e-06) * factor
        pieces.append(
            (
                jnp.where(i >= j, own_real[q], cross(turned[q], one[q])) * own,
                cross(one[q], one[1 - q]) * other,
                cross(turned[q], one[1 - q]) * other,
            )
        )
    for block, (first, second) in enumerate(zip(*pieces)):
        rows = slice(block * count, (block + 1) * count)
        own_ref[rows] = jnp.where(h == 0, first, second)
        other_ref[rows] = jnp.where(h == 0, second, first)
    for y_ref in (own_ref, other_ref):
        y_ref[3 * count :] = jnp.broadcast_to(depth, (EXTRA, count))


def interleave(own, other, h):
    first = jnp.where(h == 0, own, other)
    second = jnp.where(h == 0, other, own)
    width = own.shape[1]
    step = width // 4
    block = lax.broadcasted_iota(jnp.int32, own.shape, 1) // step

    def by(x, blocks):
        return x if blocks == 0 else pltpu.roll(x, blocks * step % width, 1)

    def choose(a, b, c, d):
        return jnp.where(block < 2, jnp.where(block == 0, a, b), jnp.where(block == 2, c, d))

    low = choose(first, by(second, 1), by(first, 1), by(second, 2))
    high = choose(by(first, 2), by(second, 3), by(first, 3), second)
    return jnp.concatenate([low, high], axis=1)


def unfold(own_ref, other_ref, y_ref):
    peers, rows, _ = y_ref.shape
    dates = rows // 4
    count = peers * dates
    h = lax.axis_index("date") % 8 // 4
    i = lax.broadcasted_iota(jnp.int32, (count, count), 0)
    j = lax.broadcasted_iota(jnp.int32, (count, count), 1)
    for piece, x_ref in enumerate((own_ref, other_ref)):
        x = x_ref[:count]
        depth = x_ref[3 * count : 3 * count + 1]
        flipped = x.T
        real = jnp.where(i >= j, x, flipped)
        imag = jnp.where(i > j, -flipped, jnp.where(i == j, depth, x))
        real = interleave(real, x_ref[count : 2 * count], h)
        imag = interleave(imag, x_ref[2 * count : 3 * count], h)
        first = piece * 2 * dates
        real = real.reshape(peers, dates, 2 * count)
        imag = imag.reshape(peers, dates, 2 * count)
        for place, peer in enumerate(SEATS):
            y_ref[place, first : first + dates] = real[peer]
            y_ref[place, first + dates : first + 2 * dates] = imag[peer]


def spread(x_ref, y_ref):
    looks, both, count = x_ref.shape
    dates = both // 2
    tile, date = lax.axis_index("tile"), lax.axis_index("date")
    h = date % 8 // 4
    rows = []
    for look in range(looks):
        source, piece = found_at(look, tile, h)
        rows.append(x_ref[source * 2 + piece])
    x = jnp.stack(rows)
    shape = (looks, dates, count)
    i = lax.broadcasted_iota(jnp.int32, shape, 1)
    j = lax.broadcasted_iota(jnp.int32, shape, 2)
    own = j == i + date * dates
    imag = x[:, dates:]
    depth = jnp.sum(jnp.where(own, imag, 0.0), axis=2, keepdims=True)
    scale = jnp.exp2(-SHIFT - depth)
    y_ref[0] = jnp.swapaxes(x[:, :dates] * scale, 0, 1)
    y_ref[1] = jnp.swapaxes(jnp.where(own, 0.0, imag * scale), 0, 1)


def call(kernel, out_shape, *xs):
    return pl.pallas_call(
        kernel,
        out_shape=out_shape,
        in_specs=[VMEM] * len(xs),
        out_specs=jax.tree.map(lambda _: VMEM, out_shape),
        compiler_params=pltpu.CompilerParams(vmem_limit_bytes=32 * 1024 * 1024),
    )(*xs)


def on_device(slc):
    parts, dates, rows, cols = slc.shape
    blocks = lax.axis_size("date")
    pixels = LOOK_ROWS * LOOK_COLS
    count = blocks * dates
    x = slc.transpose(0, 1, 3, 2)
    x = call(split_looks, jax.ShapeDtypeStruct((blocks, parts * dates, pixels), jnp.bfloat16), x)
    x = lax.all_to_all(x, "date", 0, 0, axis_index_groups=[middle_first()], tiled=True)
    shape = jax.ShapeDtypeStruct((3 * count // 2 + EXTRA, count // 2), jnp.float32)
    own, other = call(pairs, (shape, shape), x)
    other = lax.ppermute(other.astype(jnp.float16), ("date", "tile"), moves(False))
    own = lax.ppermute(own.astype(jnp.float16), ("date", "tile"), moves(True))
    x = call(
        unfold,
        jax.ShapeDtypeStruct((blocks // 2, 2 * parts * dates, count), jnp.float32),
        own.astype(jnp.float32),
        other.astype(jnp.float32),
    )
    x = lax.all_to_all(x.astype(jnp.float16), "date", 0, 0, axis_index_groups=quads(), tiled=True)
    x = x.astype(jnp.float32).reshape(blocks, parts * dates, count)
    return call(spread, jax.ShapeDtypeStruct((parts, dates, blocks, count), jnp.float32), x)


def solution(mesh):
    in_specs = (P(None, "date", None, "tile"),)
    out_specs = P(None, "date", "tile", None)
    return jax.shard_map(
        on_device, mesh=mesh, in_specs=in_specs, out_specs=out_specs, check_vma=False
    )
```
